768 devices in a mesh: term: 64 (over x, y, core), sector: 12 (over z).
Axes of the slice: x: 4, y: 8, z: 12, core: 2. Of those that a mesh axis runs over, the one named last changes fastest.
Arguments:
- psi: bfloat16 [12, 512, 512], P('sector', 'term'), may hold values from -6 to 6
- sizes: int32 [12], P('sector'), may hold values from 128 to 512, as said below
- left_ops: bfloat16 [256, 12, 512, 512], P('term', 'sector'), may hold values from -0.015625 to 0.015625
- right_ops: bfloat16 [256, 12, 512, 512], P('term', 'sector'), may hold values from -0.25 to 0.25
- source: int32 [256, 12], P('term', 'sector'), may hold values from 0 to 11
Outputs:
- sigma: bfloat16 [512, 12, 512], P('term', 'sector')
The draws below stay inside these ranges and needn't reach their ends.
Inputs may be any that keep to these rules, and one draw needn't show every extreme that they name: `sizes`: each is a multiple of 128; some sector has the full 512.
All inputs are finite; a program needn't handle non-finite values.
Results may differ from the reference program's by a relative error of at most 0.0049.
Values may be sent and summed in bfloat16 or wider, within the bound.
No kernel may reach another device: no remote copies, remote signals or barrier semaphores. Data moves between devices by JAX's collectives and lax.ppermute only.
A program may use at most 32 MiB of HBM per device.

```python
import jax
import jax.numpy as jnp
from jax import lax

B = 512
NSEC = 12
TERMS = 256


def draw_sizes(key, part):
    key = jax.random.fold_in(key, 1)
    levels = jax.random.randint(key, (NSEC,), 1, 5).astype(jnp.int32)
    levels = levels.at[0].set(4)
    return levels * (B // 4)


def plant(result, rng, smallest, largest):
    shape = result.shape
    index_at = [jax.random.randint(jax.random.fold_in(rng, axis), (), 0, shape[axis]) for axis in range(len(shape))]
    result = result.at[tuple(index_at)].set(smallest)
    longest = shape.index(max(shape))
    index_at[longest] = (index_at[longest] + 1) % shape[longest]
    return result.at[tuple(index_at)].set(largest)


def block_scale(rng, shape, shards, least, largest):
    factor_of = 1.0
    for dim, blocks in shards:
        draws = jax.random.uniform(jax.random.fold_in(jax.random.fold_in(rng, 6), dim), (blocks,), jnp.float32, least / len(shards), largest / len(shards))
        factor_of = factor_of * jnp.repeat(jnp.exp(draws), shape[dim] // blocks).reshape((-1,) + (1,) * (len(shape) - 1 - dim))
    return factor_of


def noise(rng, dims, spread, most, cuts=(), kind=jnp.bfloat16):
    result = jax.random.normal(rng, dims, jnp.float32) * spread
    if len(cuts) > 0:
        result = block_scale(rng, dims, cuts, -0.22, 0.18) * result
    return jnp.clip(result, min=-most, max=most).astype(kind)


def setup_inputs(seed: int = 0) -> dict:
    streams_of = jax.random.split(jax.random.key(seed), 6)
    return {
        "psi": noise(streams_of[0], (NSEC, B, B), 1.0, 6.0, ((0, 12), (1, 64))),
        "sizes": draw_sizes(jax.random.fold_in(streams_of[5], 71), 0),
        "left_ops": noise(streams_of[2], (TERMS, NSEC, B, B), (B * TERMS) ** -0.5, 0.015625, ((0, 64), (1, 12))),
        "right_ops": noise(streams_of[3], (TERMS, NSEC, B, B), B ** -0.5, 0.25, ((0, 64), (1, 12))),
        "source": plant(jax.random.randint(streams_of[4], (TERMS, NSEC), 0, NSEC), jax.random.fold_in(streams_of[4], 1), 0, NSEC - 1).astype(jnp.int32),
    }


def reference(psi, sizes, left_ops, right_ops, source):
    block_size = psi.shape[1]
    positions = jnp.arange(block_size, dtype=jnp.int32)
    inside = (positions[None, :, None] < sizes[:, None, None]) & (positions[None, None, :] < sizes[:, None, None])
    masked = jnp.where(inside, psi, jnp.zeros((), psi.dtype))

    def one_sector(sector):
        lefts = lax.dynamic_index_in_dim(left_ops, sector, 1, keepdims=False)
        rights = lax.dynamic_index_in_dim(right_ops, sector, 1, keepdims=False)
        wanted = lax.dynamic_index_in_dim(source, sector, 1, keepdims=False)
        chosen = masked[wanted]
        product = jnp.einsum("kab,kbc->kac", chosen.astype(jnp.float32), rights.astype(jnp.float32)).astype(jnp.bfloat16)
        total = jnp.einsum("kab,kbc->ac", lefts.astype(jnp.float32), product.astype(jnp.float32))
        bound = sizes[sector]
        keep = (positions[:, None] < bound) & (positions[None, :] < bound)
        return jnp.where(keep, total, jnp.float32(0.0))

    sigma = lax.map(one_sector, jnp.arange(NSEC, dtype=jnp.int32))
    return jnp.transpose(sigma, (1, 0, 2)).astype(jnp.bfloat16)
```

```python
import functools

import jax
import jax.numpy as jnp
from jax import lax
from jax.experimental import pallas as pl
from jax.experimental.pallas import tpu as pltpu
from jax.sharding import Mesh
from jax.sharding import PartitionSpec as P

NX, NY, NC, NZ = 4, 8, 2, 12
B = 512
ROWS = 8
HALF = B // 2
PART = HALF // NX
ORDER = (0, 2, 4, 6, 1, 3, 5, 7)
CHIP = ("x", "y")
ALL = ("x", "y", "c", "z")


def diagonal_groups():
    return [[((a - z) % NX) * NZ + z for z in range(NZ)] for a in range(NX)]


def plane_groups():
    return [[((h - 2 * y) % NX) * NY + y for y in ORDER] for h in range(NX)]


def shifts(core0, core1):
    pairs = []
    for x in range(NX):
        for y in range(NY):
            for c in range(NC):
                for z in range(NZ):
                    dx, dy, dz = core0 if c == 0 else core1
                    at = ((x * NY + y) * NC + c) * NZ + z
                    come = (((x + dx) % NX * NY + (y + dy) % NY) * NC + c) * NZ + (z + dz) % NZ
                    pairs.append((come, at))
    return pairs


def split_columns(core_ref, left_ref, own_ref, other_ref):
    core = core_ref[0]
    row = lax.broadcasted_iota(jnp.int32, (B, B), 0)
    col = lax.broadcasted_iota(jnp.int32, (B, B), 1)
    where_from = (
        ((col >> 6) & 3) * 128
        + ((col >> 3) & 3) * 32
        + ((col >> 5) & 1) * 16
        + (((col >> 8) & 1) ^ core) * 8
        + (col & 7)
    )
    pick = jnp.where(row == where_from, 1.0, 0.0).astype(jnp.bfloat16)
    moved = jnp.dot(left_ref[0], pick, preferred_element_type=jnp.float32).astype(jnp.bfloat16)
    own_ref[0] = moved[:, :HALF]
    other_ref[0] = moved[:, HALF:]


def matvec(
    wanted_ref,
    at_ref,
    a0,
    a1,
    a2,
    a3,
    b0,
    b1,
    b2,
    b3,
    right_a,
    right_b,
    left_a,
    left_b,
    keep_ref,
    send_ref,
    total,
    product_a,
    product_b,
):
    step = pl.program_id(0)

    def one(parts, right, left, product, slot):
        start = at_ref[0] + 16 - wanted_ref[slot]
        rows = jnp.concatenate([p[...].reshape(PART, B) for p in parts], axis=0)
        result = jnp.dot(rows, right[0], preferred_element_type=jnp.float32).astype(jnp.bfloat16)
        for q in range(4):
            for odd in range(2):
                piece = result[q * PART + odd * 32 : q * PART + odd * 32 + 32]
                product[(start + q - 2 * odd) & 3, odd] = piece
        return jnp.dot(
            left[0], product[...].reshape(HALF, B), preferred_element_type=jnp.float32
        )

    both = one((a0, a1, a2, a3), right_a, left_a, product_a, step) + one(
        (b0, b1, b2, b3), right_b, left_b, product_b, step + 4
    )

    @pl.when(step == 0)
    def _():
        total[...] = both

    @pl.when(step > 0)
    def _():
        total[...] += both

    @pl.when(step == pl.num_programs(0) - 1)
    def _():
        pairs = total[...].reshape(NX * NY, 2, ROWS, B)
        low, high = pairs[:, 0], pairs[:, 1]
        first = at_ref[1] == 0
        keep_ref[...] = jnp.where(first, low, high)
        send_ref[...] = jnp.where(first, high, low).astype(jnp.bfloat16)


def on_device(psi, sizes, left_ops, right_ops, source):
    x, y, c, z = (lax.axis_index(a) for a in ALL)
    term_count = left_ops.shape[0]
    swap = [(0, 1), (1, 0)]
    left = left_ops.reshape(term_count, B, B)
    right = right_ops.reshape(term_count, B, B)
    wanted = source.reshape(term_count)

    own_rows = ((x * NY + y) * NC + c) * ROWS + jnp.arange(ROWS, dtype=jnp.int32)
    columns = jnp.arange(B, dtype=jnp.int32)
    inside = (own_rows[:, None] < sizes[0]) & (columns[None, :] < sizes[0])
    masked = jnp.where(inside, psi[0], jnp.zeros((), psi.dtype))

    core = c.astype(jnp.int32).reshape(1)
    left_own, left_other = pl.pallas_call(
        split_columns,
        grid_spec=pltpu.PrefetchScalarGridSpec(
            num_scalar_prefetch=1,
            grid=(term_count,),
            in_specs=[pl.BlockSpec((1, B, B), lambda k, core: (k, 0, 0))],
            out_specs=[pl.BlockSpec((1, B, HALF), lambda k, core: (k, 0, 0))] * 2,
        ),
        out_shape=[jax.ShapeDtypeStruct((term_count, B, HALF), jnp.bfloat16)] * 2,
        cost_estimate=pl.CostEstimate(flops=2 * term_count * B**3, bytes_accessed=4 * term_count * B * B, transcendentals=0),
    )(core, left)
    right_far = lax.ppermute(right, "c", swap)
    left_far = lax.ppermute(left_other, "c", swap)
    wanted_far = lax.ppermute(wanted, "c", swap)

    by_sector = lax.all_to_all(
        jnp.broadcast_to(masked[None], (NZ, ROWS, B)),
        ("x", "z"),
        0,
        0,
        axis_index_groups=diagonal_groups(),
        tiled=True,
    )
    part = lax.all_to_all(
        jnp.broadcast_to(by_sector[None], (NY, NZ, ROWS, B)),
        CHIP,
        0,
        0,
        axis_index_groups=plane_groups(),
        tiled=True,
    )
    part = part.transpose(1, 0, 2, 3).reshape(NZ, PART, B)
    up = lax.ppermute(part, ALL, shifts((1, 0, 0), (0, 0, 1)))
    down = lax.ppermute(part, ALL, shifts((-1, 0, 0), (0, 0, -1)))
    across = lax.ppermute(part, ALL, shifts((0, 1, 0), (0, -1, 0)))
    parts = (part, up, across, down)

    near = [pl.BlockSpec((1, PART, B), lambda k, w, at: (w[k], 0, 0))] * 4
    far = [pl.BlockSpec((1, PART, B), lambda k, w, at: (w[k + 4], 0, 0))] * 4
    whole = pl.BlockSpec((1, B, B), lambda k, w, at: (k, 0, 0))
    halved = pl.BlockSpec((1, B, HALF), lambda k, w, at: (k, 0, 0))
    result = pl.BlockSpec((NX * NY, ROWS, B), lambda k, w, at: (0, 0, 0))
    keep, send = pl.pallas_call(
        matvec,
        grid_spec=pltpu.PrefetchScalarGridSpec(
            num_scalar_prefetch=2,
            grid=(term_count,),
            in_specs=near + far + [whole, whole, halved, halved],
            out_specs=[result, result],
            scratch_shapes=[
                pltpu.VMEM((B, B), jnp.float32),
                pltpu.VMEM((4, 2, 32, B), jnp.bfloat16),
                pltpu.VMEM((4, 2, 32, B), jnp.bfloat16),
            ],
        ),
        out_shape=[
            jax.ShapeDtypeStruct((NX * NY, ROWS, B), jnp.float32),
            jax.ShapeDtypeStruct((NX * NY, ROWS, B), jnp.bfloat16),
        ],
        compiler_params=pltpu.CompilerParams(vmem_limit_bytes=32 * 1024 * 1024),
        cost_estimate=pl.CostEstimate(flops=8 * term_count * HALF * B * B, bytes_accessed=16 * term_count * HALF * B, transcendentals=0),
    )(
        jnp.concatenate([wanted, wanted_far]),
        jnp.stack([(x + 2 * y + z).astype(jnp.int32), c.astype(jnp.int32)]),
        *parts,
        *parts,
        right,
        right_far,
        left_own,
        left_far,
    )
    chip_sum = keep + lax.ppermute(send, "c", swap).astype(jnp.float32)
    shares = lax.all_to_all(chip_sum.astype(jnp.bfloat16), CHIP, 0, 0, tiled=True)
    summed = jnp.sum(shares.astype(jnp.float32), axis=0)
    return jnp.where(inside, summed, jnp.float32(0.0)).astype(jnp.bfloat16)[:, None, :]


def solution(mesh):
    fine = Mesh(mesh.devices.reshape(NX, NY, NC, NZ), ALL)
    term = ("x", "y", "c")
    return jax.shard_map(
        on_device,
        mesh=fine,
        in_specs=(
            P("z", term, None),
            P("z"),
            P(term, "z", None, None),
            P(term, "z", None, None),
            P(term, "z"),
        ),
        out_specs=P(term, "z", None),
        check_vma=False,
    )
```

```python
import functools

import jax
import jax.numpy as jnp
from jax import lax
from jax.experimental import pallas as pl
from jax.experimental.pallas import tpu as pltpu
from jax.sharding import Mesh
from jax.sharding import PartitionSpec as P

NX, NY, NC, NZ = 4, 8, 2, 12
B = 512
ROWS = 8
HALF = B // 2
UNIT = 2 * ROWS
CHIP = ("x", "y")
ALL = ("x", "y", "c", "z")


def far_groups():
    return [
        [((g - z) % 4 + 4 * half) * NZ + z for z in range(NZ) for half in range(2)]
        for g in range(4)
    ]


def near_groups():
    return [
        [(x * NY + (y + x % 2) % NY) * NZ + (z + x % 2) % NZ for x in range(NX)]
        for y in range(NY)
        for z in range(NZ)
    ]


def shifts(core0, core1):
    pairs = []
    for x in range(NX):
        for y in range(NY):
            for c in range(NC):
                for z in range(NZ):
                    dx, dy, dz = core0 if c == 0 else core1
                    at = ((x * NY + y) * NC + c) * NZ + z
                    come = (((x + dx) % NX * NY + (y + dy) % NY) * NC + c) * NZ + (z + dz) % NZ
                    pairs.append((come, at))
    return pairs


def split_columns(core_ref, left_ref, own_ref, other_ref):
    core = core_ref[0]
    row = lax.broadcasted_iota(jnp.int32, (B, B), 0)
    col = lax.broadcasted_iota(jnp.int32, (B, B), 1)
    where_from = (
        ((col >> 6) & 3) * 128
        + ((col >> 3) & 1) * 64
        + ((col >> 4) & 3) * 16
        + (((col >> 8) & 1) ^ core) * 8
        + (col & 7)
    )
    pick = jnp.where(row == where_from, 1.0, 0.0).astype(jnp.bfloat16)
    moved = jnp.dot(left_ref[0], pick, preferred_element_type=jnp.float32).astype(jnp.bfloat16)
    own_ref[...] = moved[:, :HALF]
    other_ref[...] = moved[:, HALF:]


def partial_sum(
    quarters, wanted_ref, wanted_far_ref, at_ref, parts, right_ref, right_far_ref, left_ref, left_far_ref, product
):
    terms = right_ref.shape[0]
    rest = [q for q in range(4) if q not in quarters]
    zeros = jnp.zeros((UNIT, B), jnp.bfloat16)

    def multiply(sector, right, slot):
        start = at_ref[0] + 16 - sector
        rows = jnp.concatenate([p[x, sector] for p in parts for x in range(NX)], axis=0)
        result = jnp.dot(rows, right, preferred_element_type=jnp.float32).astype(jnp.bfloat16)
        base = slot * (HALF // UNIT)
        for i, q in enumerate(quarters):
            for x in range(NX):
                at = (i * NX + x) * UNIT
                product[base + x * 4 + ((start + q - 2 * x) & 3)] = result[at : at + UNIT]
        for q in rest:
            for x in range(NX):
                product[base + x * 4 + ((start + q - 2 * x) & 3)] = zeros

    for k in range(terms):
        multiply(wanted_ref[k], right_ref[k], k)
        multiply(wanted_far_ref[k], right_far_ref[k], terms + k)
    middle = terms * HALF // UNIT
    return jnp.dot(
        left_ref[...],
        product[:middle].reshape(terms * HALF, B),
        preferred_element_type=jnp.float32,
    ) + jnp.dot(
        left_far_ref[...],
        product[middle:].reshape(terms * HALF, B),
        preferred_element_type=jnp.float32,
    )


def early_sum(
    wanted_ref, wanted_far_ref, at_ref, part0, part3, right_ref, right_far_ref, left_ref, left_far_ref, total_ref, product
):
    total_ref[...] = partial_sum(
        (0, 3), wanted_ref, wanted_far_ref, at_ref, (part0, part3), right_ref, right_far_ref, left_ref, left_far_ref, product
    )


def late_sum(
    wanted_ref, wanted_far_ref, at_ref, part1, part2, right_ref, right_far_ref, left_ref, left_far_ref, early_ref, keep_ref, send_ref, product
):
    total = early_ref[...] + partial_sum(
        (1, 2), wanted_ref, wanted_far_ref, at_ref, (part1, part2), right_ref, right_far_ref, left_ref, left_far_ref, product
    )
    pairs = total.reshape(NX * NY, 2, ROWS, B)
    low, high = pairs[:, 0], pairs[:, 1]
    first = at_ref[1] == 0
    keep_ref[...] = jnp.where(first, low, high)
    send_ref[...] = jnp.where(first, high, low).astype(jnp.bfloat16)


def on_device(psi, sizes, left_ops, right_ops, source):
    x, y, c, z = (lax.axis_index(a) for a in ALL)
    term_count = left_ops.shape[0]
    swap = [(0, 1), (1, 0)]
    left = left_ops.reshape(term_count, B, B)
    right = right_ops.reshape(term_count, B, B)
    wanted = source.reshape(term_count)

    own_rows = ((x * NY + y) * NC + c) * ROWS + jnp.arange(ROWS, dtype=jnp.int32)
    columns = jnp.arange(B, dtype=jnp.int32)
    inside = (own_rows[:, None] < sizes[0]) & (columns[None, :] < sizes[0])
    masked = jnp.where(inside, psi[0], jnp.zeros((), psi.dtype))

    core = c.astype(jnp.int32).reshape(1)
    left_own, left_other = pl.pallas_call(
        split_columns,
        grid_spec=pltpu.PrefetchScalarGridSpec(
            num_scalar_prefetch=1,
            grid=(term_count,),
            in_specs=[pl.BlockSpec((1, B, B), lambda k, core: (k, 0, 0))],
            out_specs=[pl.BlockSpec((B, HALF), lambda k, core: (0, k))] * 2,
        ),
        out_shape=[jax.ShapeDtypeStruct((B, term_count * HALF), jnp.bfloat16)] * 2,
        cost_estimate=pl.CostEstimate(flops=2 * term_count * B**3, bytes_accessed=4 * term_count * B * B, transcendentals=0),
    )(core, left)
    right_far = lax.ppermute(right, "c", swap)
    wanted_far = lax.ppermute(wanted, "c", swap)

    far = lax.all_to_all(
        jnp.broadcast_to(masked[None], (2 * NZ, ROWS, B)),
        ("y", "z"),
        0,
        0,
        axis_index_groups=far_groups(),
        tiled=True,
    ).reshape(NZ, UNIT, B)
    far, left_own, left_other, wanted_far = lax.optimization_barrier(
        (far, left_own, left_other, wanted_far)
    )
    left_far = lax.ppermute(left_other, "c", swap)
    part = lax.all_to_all(
        jnp.broadcast_to(far[None], (NX, NZ, UNIT, B)),
        ("x", "y", "z"),
        0,
        0,
        axis_index_groups=near_groups(),
        tiled=True,
    )
    up = lax.ppermute(part, ALL, shifts((0, 1, 0), (0, 0, 1)))
    down = lax.ppermute(part, ALL, shifts((0, -1, 0), (0, 0, -1)))
    across = lax.ppermute(part, ALL, shifts((1, 0, 0), (-1, 0, 0)))

    in_smem = pl.BlockSpec(memory_space=pltpu.SMEM)
    in_vmem = pl.BlockSpec(memory_space=pltpu.VMEM)
    settings = dict(
        scratch_shapes=[pltpu.VMEM((2 * term_count * HALF // UNIT, UNIT, B), jnp.bfloat16)],
        compiler_params=pltpu.CompilerParams(vmem_limit_bytes=16 * 1024 * 1024),
        cost_estimate=pl.CostEstimate(
            flops=4 * term_count * HALF * B * B,
            bytes_accessed=16 * term_count * HALF * B,
            transcendentals=0,
        ),
    )
    at = jnp.stack([(2 * x + y + z).astype(jnp.int32), c.astype(jnp.int32)])
    early = pl.pallas_call(
        early_sum,
        in_specs=[in_smem] * 3 + [in_vmem] * 6,
        out_specs=in_vmem,
        out_shape=jax.ShapeDtypeStruct((B, B), jnp.float32),
        **settings,
    )(wanted, wanted_far, at, part, down, right, right_far, left_own, left_far)
    keep, send = pl.pallas_call(
        late_sum,
        in_specs=[in_smem] * 3 + [in_vmem] * 7,
        out_specs=[in_vmem] * 2,
        out_shape=[
            jax.ShapeDtypeStruct((NX * NY, ROWS, B), jnp.float32),
            jax.ShapeDtypeStruct((NX * NY, ROWS, B), jnp.bfloat16),
        ],
        **settings,
    )(wanted, wanted_far, at, up, across, right, right_far, left_own, left_far, early)
    chip_sum = keep + lax.ppermute(send, "c", swap).astype(jnp.float32)
    shares = lax.all_to_all(chip_sum.astype(jnp.bfloat16), CHIP, 0, 0, tiled=True)
    summed = jnp.sum(shares.astype(jnp.float32), axis=0)
    return jnp.where(inside, summed, jnp.float32(0.0)).astype(jnp.bfloat16)[:, None, :]


def solution(mesh):
    fine = Mesh(mesh.devices.reshape(NX, NY, NC, NZ), ALL)
    term = ("x", "y", "c")
    return jax.shard_map(
        on_device,
        mesh=fine,
        in_specs=(
            P("z", term, None),
            P("z"),
            P(term, "z", None, None),
            P(term, "z", None, None),
            P(term, "z"),
        ),
        out_specs=P(term, "z", None),
        check_vma=False,
    )
```

```python
import functools

import jax
import jax.numpy as jnp
from jax import lax
from jax.experimental import pallas as pl
from jax.experimental.pallas import tpu as pltpu
from jax.sharding import Mesh
from jax.sharding import PartitionSpec as P

NX, NY, NC, NZ = 4, 8, 2, 12
B = 512
ROWS = 8
HALF = B // 2
UNIT = 2 * ROWS
CHIP = ("x", "y")
ALL = ("x", "y", "c", "z")


def far_groups():
    return [
        [((g - z) % 4 + 4 * half) * NZ + z for z in range(NZ) for half in range(2)]
        for g in range(4)
    ]


def near_groups():
    return [
        [(x * NY + (y + x % 2) % NY) * NZ + (z + x % 2) % NZ for x in range(NX)]
        for y in range(NY)
        for z in range(NZ)
    ]


def shifts(core0, core1):
    pairs = []
    for x in range(NX):
        for y in range(NY):
            for c in range(NC):
                for z in range(NZ):
                    dx, dy, dz = core0 if c == 0 else core1
                    at = ((x * NY + y) * NC + c) * NZ + z
                    come = (((x + dx) % NX * NY + (y + dy) % NY) * NC + c) * NZ + (z + dz) % NZ
                    pairs.append((come, at))
    return pairs


def split_columns(core_ref, left_ref, own_ref, other_ref):
    core = core_ref[0]
    row = lax.broadcasted_iota(jnp.int32, (B, B), 0)
    col = lax.broadcasted_iota(jnp.int32, (B, B), 1)
    where_from = (
        ((col >> 6) & 3) * 128
        + ((col >> 3) & 1) * 64
        + ((col >> 4) & 3) * 16
        + (((col >> 8) & 1) ^ core) * 8
        + (col & 7)
    )
    pick = jnp.where(row == where_from, 1.0, 0.0).astype(jnp.bfloat16)
    moved = jnp.dot(left_ref[0], pick, preferred_element_type=jnp.float32).astype(jnp.bfloat16)
    own_ref[...] = moved[:, :HALF]
    other_ref[...] = moved[:, HALF:]


def multiply(quarters, parts, sector, start, right, product, slot):
    rows = jnp.concatenate([p[x, sector] for p in parts for x in range(NX)], axis=0)
    result = jnp.dot(rows, right, preferred_element_type=jnp.float32).astype(jnp.bfloat16)
    for i, q in enumerate(quarters):
        for x in range(NX):
            at = (i * NX + x) * UNIT
            place = slot * (HALF // UNIT) + x * 4 + ((start + q - 2 * x) & 3)
            product[place] = result[at : at + UNIT]


def early_products(
    wanted_ref,
    wanted_far_ref,
    at_ref,
    part0,
    part3,
    right_ref,
    right_far_ref,
    left_ref,
    left_far_ref,
    product_ref,
    right_far,
    left,
    left_far,
    sems,
):
    fetches = [
        pltpu.make_async_copy(right_far_ref, right_far, sems.at[0]),
        pltpu.make_async_copy(left_ref, left, sems.at[1]),
        pltpu.make_async_copy(left_far_ref, left_far, sems.at[2]),
    ]
    for fetch in fetches:
        fetch.start()
    terms = right_ref.shape[0]
    for k in range(terms):
        sector = wanted_ref[k]
        start = at_ref[0] + 16 - sector
        multiply((0, 3), (part0, part3), sector, start, right_ref[k], product_ref, k)
    fetches[0].wait()
    for k in range(terms):
        sector = wanted_far_ref[k]
        start = at_ref[0] + 16 - sector
        multiply((0, 3), (part0, part3), sector, start, right_far[k], product_ref, terms + k)
    fetches[1].wait()
    fetches[2].wait()


def late_sum(
    wanted_ref,
    wanted_far_ref,
    at_ref,
    part1,
    part2,
    right_ref,
    right_far_ref,
    left_ref,
    left_far_ref,
    early_ref,
    product_ref,
    keep_ref,
    send_ref,
):
    terms = right_ref.shape[0]
    for k in range(terms):
        for sector, right, slot in (
            (wanted_ref[k], right_ref[k], k),
            (wanted_far_ref[k], right_far_ref[k], terms + k),
        ):
            start = at_ref[0] + 16 - sector
            multiply((1, 2), (part1, part2), sector, start, right, product_ref, slot)
    middle = terms * HALF // UNIT
    total = jnp.dot(
        left_ref[...],
        product_ref[:middle].reshape(terms * HALF, B),
        preferred_element_type=jnp.float32,
    ) + jnp.dot(
        left_far_ref[...],
        product_ref[middle:].reshape(terms * HALF, B),
        preferred_element_type=jnp.float32,
    )
    row = lax.broadcasted_iota(jnp.int32, (B, B), 0)
    col = lax.broadcasted_iota(jnp.int32, (B, B), 1)
    total = jnp.where((row < at_ref[2]) & (col < at_ref[2]), total, 0.0)
    pairs = total.reshape(NX * NY, 2, ROWS, B)
    low, high = pairs[:, 0], pairs[:, 1]
    first = at_ref[1] == 0
    keep_ref[...] = jnp.where(first, low, high)
    send_ref[...] = jnp.where(first, high, low).astype(jnp.bfloat16)


def on_device(psi, sizes, left_ops, right_ops, source):
    x, y, c, z = (lax.axis_index(a) for a in ALL)
    term_count = left_ops.shape[0]
    swap = [(0, 1), (1, 0)]
    left = left_ops.reshape(term_count, B, B)
    right = right_ops.reshape(term_count, B, B)
    wanted = source.reshape(term_count)

    shape = (2 * NZ, ROWS, B)
    row = ((x * NY + y) * NC + c) * ROWS + lax.broadcasted_iota(jnp.int32, shape, 1)
    col = lax.broadcasted_iota(jnp.int32, shape, 2)
    masked = jnp.where(
        (row < sizes[0]) & (col < sizes[0]),
        jnp.broadcast_to(psi, shape),
        jnp.zeros((), psi.dtype),
    )

    core = c.astype(jnp.int32).reshape(1)
    left_own, left_other = pl.pallas_call(
        split_columns,
        grid_spec=pltpu.PrefetchScalarGridSpec(
            num_scalar_prefetch=1,
            grid=(term_count,),
            in_specs=[pl.BlockSpec((1, B, B), lambda k, core: (k, 0, 0))],
            out_specs=[pl.BlockSpec((B, HALF), lambda k, core: (0, k))] * 2,
        ),
        out_shape=[jax.ShapeDtypeStruct((B, term_count * HALF), jnp.bfloat16)] * 2,
        cost_estimate=pl.CostEstimate(flops=2 * term_count * B**3, bytes_accessed=4 * term_count * B * B, transcendentals=0),
    )(core, left)
    right_far = lax.ppermute(right, "c", swap)
    wanted_far = lax.ppermute(wanted, "c", swap)

    far = lax.all_to_all(
        masked,
        ("y", "z"),
        0,
        0,
        axis_index_groups=far_groups(),
        tiled=True,
    ).reshape(NZ, UNIT, B)
    far, left_own, left_other, wanted_far = lax.optimization_barrier(
        (far, left_own, left_other, wanted_far)
    )
    left_far = lax.ppermute(left_other, "c", swap)
    part = lax.all_to_all(
        jnp.broadcast_to(far[None], (NX, NZ, UNIT, B)),
        ("x", "y", "z"),
        0,
        0,
        axis_index_groups=near_groups(),
        tiled=True,
    )
    up = lax.ppermute(part, ALL, shifts((0, 1, 0), (0, 0, 1)))
    down = lax.ppermute(part, ALL, shifts((0, -1, 0), (0, 0, -1)))
    across = lax.ppermute(part, ALL, shifts((1, 0, 0), (-1, 0, 0)))

    in_smem = pl.BlockSpec(memory_space=pltpu.SMEM)
    in_vmem = pl.BlockSpec(memory_space=pltpu.VMEM)
    in_any = pl.BlockSpec(memory_space=pl.ANY)
    settings = dict(
        compiler_params=pltpu.CompilerParams(vmem_limit_bytes=16 * 1024 * 1024),
        cost_estimate=pl.CostEstimate(
            flops=4 * term_count * HALF * B * B,
            bytes_accessed=16 * term_count * HALF * B,
            transcendentals=0,
        ),
    )
    at = jnp.stack([(2 * x + y + z).astype(jnp.int32), c.astype(jnp.int32), sizes[0]])
    product_shape = jax.ShapeDtypeStruct((2 * term_count * HALF // UNIT, UNIT, B), jnp.bfloat16)
    left_shape = jax.ShapeDtypeStruct((B, term_count * HALF), jnp.bfloat16)
    early, right_far, left_own, left_far = pl.pallas_call(
        early_products,
        in_specs=[in_smem] * 3 + [in_vmem] * 3 + [in_any] * 3,
        out_specs=[in_vmem] * 4,
        out_shape=[
            product_shape,
            jax.ShapeDtypeStruct((term_count, B, B), jnp.bfloat16),
            left_shape,
            left_shape,
        ],
        scratch_shapes=[pltpu.SemaphoreType.DMA((3,))],
        **settings,
    )(wanted, wanted_far, at, part, down, right, right_far, left_own, left_far)
    _, keep, send = pl.pallas_call(
        late_sum,
        in_specs=[in_smem] * 3 + [in_vmem] * 7,
        out_specs=[in_vmem] * 3,
        out_shape=[
            product_shape,
            jax.ShapeDtypeStruct((NX * NY, ROWS, B), jnp.float32),
            jax.ShapeDtypeStruct((NX * NY, ROWS, B), jnp.bfloat16),
        ],
        input_output_aliases={9: 0},
        **settings,
    )(wanted, wanted_far, at, up, across, right, right_far, left_own, left_far, early)
    chip_sum = keep + lax.ppermute(send, "c", swap).astype(jnp.float32)
    shares = lax.all_to_all(chip_sum.astype(jnp.bfloat16), CHIP, 0, 0, tiled=True)
    return jnp.sum(shares[:, :, None, :].astype(jnp.float32), axis=0).astype(jnp.bfloat16)


def solution(mesh):
    fine = Mesh(mesh.devices.reshape(NX, NY, NC, NZ), ALL)
    term = ("x", "y", "c")
    return jax.shard_map(
        on_device,
        mesh=fine,
        in_specs=(
            P("z", term, None),
            P("z"),
            P(term, "z", None, None),
            P(term, "z", None, None),
            P(term, "z"),
        ),
        out_specs=P(term, "z", None),
        check_vma=False,
    )
```

```python
import functools

import jax
import jax.numpy as jnp
from jax import lax
from jax.experimental import pallas as pl
from jax.experimental.pallas import tpu as pltpu
from jax.sharding import Mesh
from jax.sharding import PartitionSpec as P

NX, NY, NC, NZ = 4, 8, 2, 12
B = 512
ROWS = 8
HALF = B // 2
UNIT = 2 * ROWS
CHIP = ("x", "y")
ALL = ("x", "y", "c", "z")


def far_groups():
    return [
        [((g - z) % 4 + 4 * half) * NZ + z for z in range(NZ) for half in range(2)]
        for g in range(4)
    ]


def near_groups():
    return [
        [(x * NY + (y + x % 2) % NY) * NZ + (z + x % 2) % NZ for x in range(NX)]
        for y in range(NY)
        for z in range(NZ)
    ]


def shifts(core0, core1):
    pairs = []
    for x in range(NX):
        for y in range(NY):
            for c in range(NC):
                for z in range(NZ):
                    dx, dy, dz = core0 if c == 0 else core1
                    at = ((x * NY + y) * NC + c) * NZ + z
                    come = (((x + dx) % NX * NY + (y + dy) % NY) * NC + c) * NZ + (z + dz) % NZ
                    pairs.append((come, at))
    return pairs


def split_columns(core_ref, left_ref, own_ref, other_ref):
    row = lax.broadcasted_iota(jnp.int32, (B, B), 0)
    col = lax.broadcasted_iota(jnp.int32, (1, B), 1)
    where_from = (
        ((col >> 6) & 3) * 128
        + ((col >> 3) & 1) * 64
        + ((col >> 4) & 3) * 16
        + (((col >> 8) & 1) ^ core_ref[0]) * 8
        + (col & 7)
    )
    pick = jnp.where(row == where_from, 1.0, 0.0).astype(jnp.bfloat16)
    for k in range(left_ref.shape[0]):
        moved = jnp.dot(left_ref[k], pick, preferred_element_type=jnp.float32).astype(jnp.bfloat16)
        columns = slice(k * HALF, k * HALF + HALF)
        own_ref[:, columns] = moved[:, :HALF]
        other_ref[:, columns] = moved[:, HALF:]


def multiply(quarters, parts, sector, start, right, product, slot):
    rows = jnp.concatenate([p[x, sector] for p in parts for x in range(NX)], axis=0)
    result = jnp.dot(rows, right, preferred_element_type=jnp.float32).astype(jnp.bfloat16)
    for i, q in enumerate(quarters):
        for x in range(NX):
            at = (i * NX + x) * UNIT
            place = slot * (HALF // UNIT) + x * 4 + ((start + q - 2 * x) & 3)
            product[place] = result[at : at + UNIT]


def early_products(
    wanted_ref,
    wanted_far_ref,
    at_ref,
    part0,
    part3,
    right_ref,
    right_far_ref,
    left_ref,
    left_far_ref,
    product_ref,
    right_far,
    left,
    left_far,
    sems,
):
    fetches = [
        pltpu.make_async_copy(right_far_ref, right_far, sems.at[0]),
        pltpu.make_async_copy(left_ref, left, sems.at[1]),
        pltpu.make_async_copy(left_far_ref, left_far, sems.at[2]),
    ]
    for fetch in fetches:
        fetch.start()
    terms = right_ref.shape[0]
    for k in range(terms):
        sector = wanted_ref[k]
        start = at_ref[0] + 16 - sector
        multiply((0, 3), (part0, part3), sector, start, right_ref[k], product_ref, k)
    fetches[0].wait()
    for k in range(terms):
        sector = wanted_far_ref[k]
        start = at_ref[0] + 16 - sector
        multiply((0, 3), (part0, part3), sector, start, right_far[k], product_ref, terms + k)
    fetches[1].wait()
    fetches[2].wait()


def late_sum(
    wanted_ref,
    wanted_far_ref,
    at_ref,
    part1,
    part2,
    right_ref,
    right_far_ref,
    left_ref,
    left_far_ref,
    early_ref,
    product_ref,
    keep_ref,
    send_ref,
):
    terms = right_ref.shape[0]
    for k in range(terms):
        for sector, right, slot in (
            (wanted_ref[k], right_ref[k], k),
            (wanted_far_ref[k], right_far_ref[k], terms + k),
        ):
            start = at_ref[0] + 16 - sector
            multiply((1, 2), (part1, part2), sector, start, right, product_ref, slot)
    middle = terms * HALF // UNIT
    total = jnp.dot(
        left_ref[...],
        product_ref[:middle].reshape(terms * HALF, B),
        preferred_element_type=jnp.float32,
    ) + jnp.dot(
        left_far_ref[...],
        product_ref[middle:].reshape(terms * HALF, B),
        preferred_element_type=jnp.float32,
    )
    row = lax.broadcasted_iota(jnp.int32, (B, B), 0)
    col = lax.broadcasted_iota(jnp.int32, (B, B), 1)
    total = jnp.where((row < at_ref[2]) & (col < at_ref[2]), total, 0.0)
    pairs = total.reshape(NX * NY, 2, ROWS, B)
    low, high = pairs[:, 0], pairs[:, 1]
    first = at_ref[1] == 0
    keep_ref[...] = jnp.where(first, low, high)
    send_ref[...] = jnp.where(first, high, low).astype(jnp.bfloat16)


def on_device(psi, sizes, left_ops, right_ops, source):
    x, y, c, z = (lax.axis_index(a) for a in ALL)
    term_count = left_ops.shape[0]
    swap = [(0, 1), (1, 0)]
    left = left_ops.reshape(term_count, B, B)
    right = right_ops.reshape(term_count, B, B)
    wanted = source.reshape(term_count)

    shape = (2 * NZ, ROWS, B)
    row = ((x * NY + y) * NC + c) * ROWS + lax.broadcasted_iota(jnp.int32, shape, 1)
    col = lax.broadcasted_iota(jnp.int32, shape, 2)
    masked = jnp.where(
        (row < sizes[0]) & (col < sizes[0]),
        jnp.broadcast_to(psi, shape),
        jnp.zeros((), psi.dtype),
    )

    core = c.astype(jnp.int32).reshape(1)
    left_own, left_other = pl.pallas_call(
        split_columns,
        in_specs=[pl.BlockSpec(memory_space=pltpu.SMEM), pl.BlockSpec(memory_space=pltpu.VMEM)],
        out_specs=[pl.BlockSpec(memory_space=pltpu.VMEM)] * 2,
        out_shape=[jax.ShapeDtypeStruct((B, term_count * HALF), jnp.bfloat16)] * 2,
        compiler_params=pltpu.CompilerParams(vmem_limit_bytes=48 * 1024 * 1024),
        cost_estimate=pl.CostEstimate(flops=2 * term_count * B**3, bytes_accessed=4 * term_count * B * B, transcendentals=0),
    )(core, left)
    right_far = lax.ppermute(right, "c", swap)
    wanted_far = lax.ppermute(wanted, "c", swap)

    far = lax.all_to_all(
        masked,
        ("y", "z"),
        0,
        0,
        axis_index_groups=far_groups(),
        tiled=True,
    ).reshape(NZ, UNIT, B)
    far, left_own, left_other, wanted_far = lax.optimization_barrier(
        (far, left_own, left_other, wanted_far)
    )
    left_far = lax.ppermute(left_other, "c", swap)
    part = lax.all_to_all(
        jnp.broadcast_to(far[None], (NX, NZ, UNIT, B)),
        ("x", "y", "z"),
        0,
        0,
        axis_index_groups=near_groups(),
        tiled=True,
    )
    up = lax.ppermute(part, ALL, shifts((0, 1, 0), (0, 0, 1)))
    down = lax.ppermute(part, ALL, shifts((0, -1, 0), (0, 0, -1)))
    across = lax.ppermute(part, ALL, shifts((1, 0, 0), (-1, 0, 0)))

    in_smem = pl.BlockSpec(memory_space=pltpu.SMEM)
    in_vmem = pl.BlockSpec(memory_space=pltpu.VMEM)
    in_any = pl.BlockSpec(memory_space=pl.ANY)
    settings = dict(
        compiler_params=pltpu.CompilerParams(vmem_limit_bytes=9 * 1024 * 1024),
        cost_estimate=pl.CostEstimate(
            flops=4 * term_count * HALF * B * B,
            bytes_accessed=16 * term_count * HALF * B,
            transcendentals=0,
        ),
    )
    at = jnp.stack([(2 * x + y + z).astype(jnp.int32), c.astype(jnp.int32), sizes[0]])
    product_shape = jax.ShapeDtypeStruct((2 * term_count * HALF // UNIT, UNIT, B), jnp.bfloat16)
    left_shape = jax.ShapeDtypeStruct((B, term_count * HALF), jnp.bfloat16)
    early, right_far, left_own, left_far = pl.pallas_call(
        early_products,
        in_specs=[in_smem] * 3 + [in_vmem] * 3 + [in_any] * 3,
        out_specs=[in_vmem] * 4,
        out_shape=[
            product_shape,
            jax.ShapeDtypeStruct((term_count, B, B), jnp.bfloat16),
            left_shape,
            left_shape,
        ],
        scratch_shapes=[pltpu.SemaphoreType.DMA((3,))],
        **settings,
    )(wanted, wanted_far, at, part, down, right, right_far, left_own, left_far)
    _, keep, send = pl.pallas_call(
        late_sum,
        in_specs=[in_smem] * 3 + [in_vmem] * 7,
        out_specs=[in_vmem] * 3,
        out_shape=[
            product_shape,
            jax.ShapeDtypeStruct((NX * NY, ROWS, B), jnp.float32),
            jax.ShapeDtypeStruct((NX * NY, ROWS, B), jnp.bfloat16),
        ],
        input_output_aliases={9: 0},
        **settings,
    )(wanted, wanted_far, at, up, across, right, right_far, left_own, left_far, early)
    chip_sum = keep + lax.ppermute(send, "c", swap).astype(jnp.float32)
    shares = lax.all_to_all(chip_sum.astype(jnp.bfloat16), CHIP, 0, 0, tiled=True)
    return jnp.sum(shares[:, :, None, :].astype(jnp.float32), axis=0).astype(jnp.bfloat16)


def solution(mesh):
    fine = Mesh(mesh.devices.reshape(NX, NY, NC, NZ), ALL)
    term = ("x", "y", "c")
    return jax.shard_map(
        on_device,
        mesh=fine,
        in_specs=(
            P("z", term, None),
            P("z"),
            P(term, "z", None, None),
            P(term, "z", None, None),
            P(term, "z"),
        ),
        out_specs=P(term, "z", None),
        check_vma=False,
    )
```

```python
import functools

import jax
import jax.numpy as jnp
from jax import lax
from jax.experimental import pallas as pl
from jax.experimental.pallas import tpu as pltpu
from jax.sharding import Mesh
from jax.sharding import PartitionSpec as P

NX, NY, NC, NZ = 4, 8, 2, 12
B = 512
ROWS = 8
HALF = B // 2
UNIT = 2 * ROWS
CHIP = ("x", "y")
ALL = ("x", "y", "c", "z")


def far_groups():
    return [
        [((g - z) % 4 + 4 * half) * NZ + z for z in range(NZ) for half in range(2)]
        for g in range(4)
    ]


def near_groups():
    return [
        [(x * NY + (y + x % 2) % NY) * NZ + (z + x % 2) % NZ for x in range(NX)]
        for y in range(NY)
        for z in range(NZ)
    ]


def shifts(core0, core1):
    pairs = []
    for x in range(NX):
        for y in range(NY):
            for c in range(NC):
                for z in range(NZ):
                    dx, dy, dz = core0 if c == 0 else core1
                    at = ((x * NY + y) * NC + c) * NZ + z
                    come = (((x + dx) % NX * NY + (y + dy) % NY) * NC + c) * NZ + (z + dz) % NZ
                    pairs.append((come, at))
    return pairs


def split_columns(core_ref, left_ref, own_ref, other_ref):
    row = lax.broadcasted_iota(jnp.int32, (B, B), 0)
    col = lax.broadcasted_iota(jnp.int32, (1, B), 1)
    where_from = (
        ((col >> 6) & 3) * 128
        + ((col >> 3) & 1) * 64
        + ((col >> 4) & 3) * 16
        + (((col >> 8) & 1) ^ core_ref[0]) * 8
        + (col & 7)
    )
    pick = jnp.where(row == where_from, 1.0, 0.0).astype(jnp.bfloat16)
    for k in range(left_ref.shape[0]):
        moved = jnp.dot(left_ref[k], pick, preferred_element_type=jnp.float32).astype(jnp.bfloat16)
        columns = slice(k * HALF, k * HALF + HALF)
        own_ref[:, columns] = moved[:, :HALF]
        other_ref[:, columns] = moved[:, HALF:]


def multiply(quarters, parts, sector, start, right, product, slot):
    rows = jnp.concatenate([p[x, sector] for p in parts for x in range(NX)], axis=0)
    result = jnp.dot(rows, right, preferred_element_type=jnp.float32).astype(jnp.bfloat16)
    for i, q in enumerate(quarters):
        for x in range(NX):
            at = (i * NX + x) * UNIT
            place = slot * (HALF // UNIT) + x * 4 + ((start + q - 2 * x) & 3)
            product[place] = result[at : at + UNIT]


def early_products(
    wanted_ref,
    wanted_far_ref,
    at_ref,
    part0,
    part3,
    right_ref,
    right_far_ref,
    left_ref,
    left_far_ref,
    product_ref,
    right_far,
    left,
    left_far,
    sems,
):
    fetches = [
        pltpu.make_async_copy(right_far_ref, right_far, sems.at[0]),
        pltpu.make_async_copy(left_ref, left, sems.at[1]),
        pltpu.make_async_copy(left_far_ref, left_far, sems.at[2]),
    ]
    for fetch in fetches:
        fetch.start()
    terms = right_ref.shape[0]
    for k in range(terms):
        sector = wanted_ref[k]
        start = at_ref[0] + 16 - sector
        multiply((0, 3), (part0, part3), sector, start, right_ref[k], product_ref, k)
    fetches[0].wait()
    for k in range(terms):
        sector = wanted_far_ref[k]
        start = at_ref[0] + 16 - sector
        multiply((0, 3), (part0, part3), sector, start, right_far[k], product_ref, terms + k)
    fetches[1].wait()
    fetches[2].wait()


def middle_products(
    wanted_ref, wanted_far_ref, at_ref, part1, right_ref, right_far_ref, early_ref, product_ref
):
    terms = right_ref.shape[0]
    for k in range(terms):
        for sector, right, slot in (
            (wanted_ref[k], right_ref[k], k),
            (wanted_far_ref[k], right_far_ref[k], terms + k),
        ):
            start = at_ref[0] + 16 - sector
            multiply((1,), (part1,), sector, start, right, product_ref, slot)


def late_sum(
    wanted_ref,
    wanted_far_ref,
    at_ref,
    part2,
    right_ref,
    right_far_ref,
    left_ref,
    left_far_ref,
    early_ref,
    product_ref,
    keep_ref,
    send_ref,
):
    terms = right_ref.shape[0]
    for k in range(terms):
        for sector, right, slot in (
            (wanted_ref[k], right_ref[k], k),
            (wanted_far_ref[k], right_far_ref[k], terms + k),
        ):
            start = at_ref[0] + 16 - sector
            multiply((2,), (part2,), sector, start, right, product_ref, slot)
    middle = terms * HALF // UNIT
    total = jnp.dot(
        left_ref[...],
        product_ref[:middle].reshape(terms * HALF, B),
        preferred_element_type=jnp.float32,
    ) + jnp.dot(
        left_far_ref[...],
        product_ref[middle:].reshape(terms * HALF, B),
        preferred_element_type=jnp.float32,
    )
    row = lax.broadcasted_iota(jnp.int32, (B, B), 0)
    col = lax.broadcasted_iota(jnp.int32, (B, B), 1)
    total = jnp.where((row < at_ref[2]) & (col < at_ref[2]), total, 0.0)
    pairs = total.reshape(NX * NY, 2, ROWS, B)
    low, high = pairs[:, 0], pairs[:, 1]
    first = at_ref[1] == 0
    keep_ref[...] = jnp.where(first, low, high)
    send_ref[...] = jnp.where(first, high, low).astype(jnp.bfloat16)


def on_device(psi, sizes, left_ops, right_ops, source):
    x, y, c, z = (lax.axis_index(a) for a in ALL)
    term_count = left_ops.shape[0]
    swap = [(0, 1), (1, 0)]
    left = left_ops.reshape(term_count, B, B)
    right = right_ops.reshape(term_count, B, B)
    wanted = source.reshape(term_count)

    shape = (2 * NZ, ROWS, B)
    row = ((x * NY + y) * NC + c) * ROWS + lax.broadcasted_iota(jnp.int32, shape, 1)
    col = lax.broadcasted_iota(jnp.int32, shape, 2)
    masked = jnp.where(
        (row < sizes[0]) & (col < sizes[0]),
        jnp.broadcast_to(psi, shape),
        jnp.zeros((), psi.dtype),
    )

    core = c.astype(jnp.int32).reshape(1)
    left_own, left_other = pl.pallas_call(
        split_columns,
        in_specs=[pl.BlockSpec(memory_space=pltpu.SMEM), pl.BlockSpec(memory_space=pltpu.VMEM)],
        out_specs=[pl.BlockSpec(memory_space=pltpu.VMEM)] * 2,
        out_shape=[jax.ShapeDtypeStruct((B, term_count * HALF), jnp.bfloat16)] * 2,
        compiler_params=pltpu.CompilerParams(vmem_limit_bytes=48 * 1024 * 1024),
        cost_estimate=pl.CostEstimate(flops=2 * term_count * B**3, bytes_accessed=4 * term_count * B * B, transcendentals=0),
    )(core, left)
    right_far = lax.ppermute(right, "c", swap)
    wanted_far = lax.ppermute(wanted, "c", swap)

    far = lax.all_to_all(
        masked,
        ("y", "z"),
        0,
        0,
        axis_index_groups=far_groups(),
        tiled=True,
    ).reshape(NZ, UNIT, B)
    far, left_own, left_other, wanted_far = lax.optimization_barrier(
        (far, left_own, left_other, wanted_far)
    )
    left_far = lax.ppermute(left_other, "c", swap)
    part = lax.all_to_all(
        jnp.broadcast_to(far[None], (NX, NZ, UNIT, B)),
        ("x", "y", "z"),
        0,
        0,
        axis_index_groups=near_groups(),
        tiled=True,
    )
    up = lax.ppermute(part, ALL, shifts((0, 1, 0), (0, 0, 1)))
    down = lax.ppermute(part, ALL, shifts((0, -1, 0), (0, 0, -1)))
    across = lax.ppermute(part, ALL, shifts((1, 0, 0), (-1, 0, 0)))

    in_smem = pl.BlockSpec(memory_space=pltpu.SMEM)
    in_vmem = pl.BlockSpec(memory_space=pltpu.VMEM)
    in_any = pl.BlockSpec(memory_space=pl.ANY)
    settings = dict(
        compiler_params=pltpu.CompilerParams(vmem_limit_bytes=9 * 1024 * 1024),
        cost_estimate=pl.CostEstimate(
            flops=4 * term_count * HALF * B * B,
            bytes_accessed=16 * term_count * HALF * B,
            transcendentals=0,
        ),
    )
    at = jnp.stack([(2 * x + y + z).astype(jnp.int32), c.astype(jnp.int32), sizes[0]])
    product_shape = jax.ShapeDtypeStruct((2 * term_count * HALF // UNIT, UNIT, B), jnp.bfloat16)
    left_shape = jax.ShapeDtypeStruct((B, term_count * HALF), jnp.bfloat16)
    early, right_far, left_own, left_far = pl.pallas_call(
        early_products,
        in_specs=[in_smem] * 3 + [in_vmem] * 3 + [in_any] * 3,
        out_specs=[in_vmem] * 4,
        out_shape=[
            product_shape,
            jax.ShapeDtypeStruct((term_count, B, B), jnp.bfloat16),
            left_shape,
            left_shape,
        ],
        scratch_shapes=[pltpu.SemaphoreType.DMA((3,))],
        **settings,
    )(wanted, wanted_far, at, part, down, right, right_far, left_own, left_far)
    middle = pl.pallas_call(
        middle_products,
        in_specs=[in_smem] * 3 + [in_vmem] * 4,
        out_specs=in_vmem,
        out_shape=product_shape,
        input_output_aliases={6: 0},
        **settings,
    )(wanted, wanted_far, at, up, right, right_far, early)
    _, keep, send = pl.pallas_call(
        late_sum,
        in_specs=[in_smem] * 3 + [in_vmem] * 6,
        out_specs=[in_vmem] * 3,
        out_shape=[
            product_shape,
            jax.ShapeDtypeStruct((NX * NY, ROWS, B), jnp.float32),
            jax.ShapeDtypeStruct((NX * NY, ROWS, B), jnp.bfloat16),
        ],
        input_output_aliases={8: 0},
        **settings,
    )(wanted, wanted_far, at, across, right, right_far, left_own, left_far, middle)
    chip_sum = keep + lax.ppermute(send, "c", swap).astype(jnp.float32)
    shares = lax.all_to_all(chip_sum.astype(jnp.bfloat16), CHIP, 0, 0, tiled=True)
    return jnp.sum(shares[:, :, None, :].astype(jnp.float32), axis=0).astype(jnp.bfloat16)


def solution(mesh):
    fine = Mesh(mesh.devices.reshape(NX, NY, NC, NZ), ALL)
    term = ("x", "y", "c")
    return jax.shard_map(
        on_device,
        mesh=fine,
        in_specs=(
            P("z", term, None),
            P("z"),
            P(term, "z", None, None),
            P(term, "z", None, None),
            P(term, "z"),
        ),
        out_specs=P(term, "z", None),
        check_vma=False,
    )
```

```python
import functools

import jax
import jax.numpy as jnp
from jax import lax
from jax.experimental import pallas as pl
from jax.experimental.pallas import tpu as pltpu
from jax.sharding import Mesh
from jax.sharding import PartitionSpec as P

NX, NY, NC, NZ = 4, 8, 2, 12
B = 512
ROWS = 8
HALF = B // 2
UNIT = 2 * ROWS
CHIP = ("y", "x")
ALL = ("x", "y", "c", "z")


def far_groups():
    return [
        [((g - z) % 4 + 4 * half) * NZ + z for z in range(NZ) for half in range(2)]
        for g in range(4)
    ]


def near_groups():
    return [
        [(x * NY + (y + x % 2) % NY) * NZ + (z + x % 2) % NZ for x in range(NX)]
        for y in range(NY)
        for z in range(NZ)
    ]


def shifts(core0, core1):
    pairs = []
    for x in range(NX):
        for y in range(NY):
            for c in range(NC):
                for z in range(NZ):
                    dx, dy, dz = core0 if c == 0 else core1
                    at = ((x * NY + y) * NC + c) * NZ + z
                    come = (((x + dx) % NX * NY + (y + dy) % NY) * NC + c) * NZ + (z + dz) % NZ
                    pairs.append((come, at))
    return pairs


def split_columns(core_ref, left_ref, own_ref, other_ref):
    row = lax.broadcasted_iota(jnp.int32, (B, B), 0)
    col = lax.broadcasted_iota(jnp.int32, (1, B), 1)
    where_from = (
        ((col >> 6) & 3) * 128
        + ((col >> 3) & 1) * 64
        + ((col >> 4) & 3) * 16
        + (((col >> 8) & 1) ^ core_ref[0]) * 8
        + (col & 7)
    )
    pick = jnp.where(row == where_from, 1.0, 0.0).astype(jnp.bfloat16)
    for k in range(left_ref.shape[0]):
        moved = jnp.dot(left_ref[k], pick, preferred_element_type=jnp.float32).astype(jnp.bfloat16)
        columns = slice(k * HALF, k * HALF + HALF)
        own_ref[:, columns] = moved[:, :HALF]
        other_ref[:, columns] = moved[:, HALF:]


def multiply(quarters, parts, sector, start, right, product, slot):
    rows = jnp.concatenate([p[x, sector] for p in parts for x in range(NX)], axis=0)
    result = jnp.dot(rows, right, preferred_element_type=jnp.float32).astype(jnp.bfloat16)
    for i, q in enumerate(quarters):
        for x in range(NX):
            at = (i * NX + x) * UNIT
            place = slot * (HALF // UNIT) + x * 4 + ((start + q - 2 * x) & 3)
            product[place] = result[at : at + UNIT]


def early_products(
    wanted_ref,
    wanted_far_ref,
    at_ref,
    part0,
    part3,
    right_ref,
    right_far_ref,
    left_ref,
    left_far_ref,
    product_ref,
    right_far,
    left,
    left_far,
    sems,
):
    fetches = [
        pltpu.make_async_copy(right_far_ref, right_far, sems.at[0]),
        pltpu.make_async_copy(left_ref, left, sems.at[1]),
        pltpu.make_async_copy(left_far_ref, left_far, sems.at[2]),
    ]
    for fetch in fetches:
        fetch.start()
    terms = right_ref.shape[0]
    for k in range(terms):
        sector = wanted_ref[k]
        start = at_ref[0] + 16 - sector
        multiply((0, 3), (part0, part3), sector, start, right_ref[k], product_ref, k)
    fetches[0].wait()
    for k in range(terms):
        sector = wanted_far_ref[k]
        start = at_ref[0] + 16 - sector
        multiply((0, 3), (part0, part3), sector, start, right_far[k], product_ref, terms + k)
    fetches[1].wait()
    fetches[2].wait()


def late_sum(
    wanted_ref,
    wanted_far_ref,
    at_ref,
    part1,
    part2,
    right_ref,
    right_far_ref,
    left_ref,
    left_far_ref,
    early_ref,
    product_ref,
    keep_ref,
    send_ref,
):
    terms = right_ref.shape[0]
    for k in range(terms):
        for sector, right, slot in (
            (wanted_ref[k], right_ref[k], k),
            (wanted_far_ref[k], right_far_ref[k], terms + k),
        ):
            start = at_ref[0] + 16 - sector
            multiply((1, 2), (part1, part2), sector, start, right, product_ref, slot)
    middle = terms * HALF // UNIT
    total = jnp.dot(
        left_ref[...],
        product_ref[:middle].reshape(terms * HALF, B),
        preferred_element_type=jnp.float32,
    ) + jnp.dot(
        left_far_ref[...],
        product_ref[middle:].reshape(terms * HALF, B),
        preferred_element_type=jnp.float32,
    )
    row = lax.broadcasted_iota(jnp.int32, (B, B), 0)
    col = lax.broadcasted_iota(jnp.int32, (B, B), 1)
    total = jnp.where((row < at_ref[2]) & (col < at_ref[2]), total, 0.0)
    pairs = jnp.swapaxes(total.reshape(NX, NY, 2, ROWS, B), 0, 1).reshape(NX * NY, 2, ROWS, B)
    low, high = pairs[:, 0], pairs[:, 1]
    first = at_ref[1] == 0
    keep_ref[...] = jnp.where(first, low, high)
    send_ref[...] = jnp.where(first, high, low).astype(jnp.bfloat16)


def on_device(psi, sizes, left_ops, right_ops, source):
    x, y, c, z = (lax.axis_index(a) for a in ALL)
    term_count = left_ops.shape[0]
    swap = [(0, 1), (1, 0)]
    left = left_ops.reshape(term_count, B, B)
    right = right_ops.reshape(term_count, B, B)
    wanted = source.reshape(term_count)

    shape = (2 * NZ, ROWS, B)
    row = ((x * NY + y) * NC + c) * ROWS + lax.broadcasted_iota(jnp.int32, shape, 1)
    col = lax.broadcasted_iota(jnp.int32, shape, 2)
    masked = jnp.where(
        (row < sizes[0]) & (col < sizes[0]),
        jnp.broadcast_to(psi, shape),
        jnp.zeros((), psi.dtype),
    )

    core = c.astype(jnp.int32).reshape(1)
    left_own, left_other = pl.pallas_call(
        split_columns,
        in_specs=[pl.BlockSpec(memory_space=pltpu.SMEM), pl.BlockSpec(memory_space=pltpu.VMEM)],
        out_specs=[pl.BlockSpec(memory_space=pltpu.VMEM)] * 2,
        out_shape=[jax.ShapeDtypeStruct((B, term_count * HALF), jnp.bfloat16)] * 2,
        compiler_params=pltpu.CompilerParams(vmem_limit_bytes=48 * 1024 * 1024),
        cost_estimate=pl.CostEstimate(flops=2 * term_count * B**3, bytes_accessed=4 * term_count * B * B, transcendentals=0),
    )(core, left)
    right_far = lax.ppermute(right, "c", swap)
    wanted_far = lax.ppermute(wanted, "c", swap)

    far = lax.all_to_all(
        masked,
        ("y", "z"),
        0,
        0,
        axis_index_groups=far_groups(),
        tiled=True,
    ).reshape(NZ, UNIT, B)
    far, left_own, left_other, wanted_far = lax.optimization_barrier(
        (far, left_own, left_other, wanted_far)
    )
    left_far = lax.ppermute(left_other, "c", swap)
    part = lax.all_to_all(
        jnp.broadcast_to(far[None], (NX, NZ, UNIT, B)),
        ("x", "y", "z"),
        0,
        0,
        axis_index_groups=near_groups(),
        tiled=True,
    )
    up = lax.ppermute(part, ALL, shifts((0, 1, 0), (0, 0, 1)))
    down = lax.ppermute(part, ALL, shifts((0, -1, 0), (0, 0, -1)))
    across = lax.ppermute(part, ALL, shifts((1, 0, 0), (-1, 0, 0)))

    in_smem = pl.BlockSpec(memory_space=pltpu.SMEM)
    in_vmem = pl.BlockSpec(memory_space=pltpu.VMEM)
    in_any = pl.BlockSpec(memory_space=pl.ANY)
    settings = dict(
        compiler_params=pltpu.CompilerParams(vmem_limit_bytes=9 * 1024 * 1024),
        cost_estimate=pl.CostEstimate(
            flops=4 * term_count * HALF * B * B,
            bytes_accessed=16 * term_count * HALF * B,
            transcendentals=0,
        ),
    )
    at = jnp.stack([(2 * x + y + z).astype(jnp.int32), c.astype(jnp.int32), sizes[0]])
    product_shape = jax.ShapeDtypeStruct((2 * term_count * HALF // UNIT, UNIT, B), jnp.bfloat16)
    left_shape = jax.ShapeDtypeStruct((B, term_count * HALF), jnp.bfloat16)
    early, right_far, left_own, left_far = pl.pallas_call(
        early_products,
        in_specs=[in_smem] * 3 + [in_vmem] * 3 + [in_any] * 3,
        out_specs=[in_vmem] * 4,
        out_shape=[
            product_shape,
            jax.ShapeDtypeStruct((term_count, B, B), jnp.bfloat16),
            left_shape,
            left_shape,
        ],
        scratch_shapes=[pltpu.SemaphoreType.DMA((3,))],
        **settings,
    )(wanted, wanted_far, at, part, down, right, right_far, left_own, left_far)
    _, keep, send = pl.pallas_call(
        late_sum,
        in_specs=[in_smem] * 3 + [in_vmem] * 7,
        out_specs=[in_vmem] * 3,
        out_shape=[
            product_shape,
            jax.ShapeDtypeStruct((NX * NY, ROWS, B), jnp.float32),
            jax.ShapeDtypeStruct((NX * NY, ROWS, B), jnp.bfloat16),
        ],
        input_output_aliases={9: 0},
        **settings,
    )(wanted, wanted_far, at, up, across, right, right_far, left_own, left_far, early)
    chip_sum = keep + lax.ppermute(send, "c", swap).astype(jnp.float32)
    shares = lax.all_to_all(chip_sum.astype(jnp.bfloat16), CHIP, 0, 0, tiled=True)
    return jnp.sum(shares[:, :, None, :].astype(jnp.float32), axis=0).astype(jnp.bfloat16)


def solution(mesh):
    fine = Mesh(mesh.devices.reshape(NX, NY, NC, NZ), ALL)
    term = ("x", "y", "c")
    return jax.shard_map(
        on_device,
        mesh=fine,
        in_specs=(
            P("z", term, None),
            P("z"),
            P(term, "z", None, None),
            P(term, "z", None, None),
            P(term, "z"),
        ),
        out_specs=P(term, "z", None),
        check_vma=False,
    )
```
